256 devices in a mesh: leaf: 16 (over x_hi, z), blk: 4 (over x_lo, core), kv: 4 (over y).
Axes of the slice: x: 4 (x_hi: 2, x_lo: 2; x = x_hi * 2 + x_lo), y: 4, z: 8, core: 2. Of those that a mesh axis runs over, the one named last changes fastest.
Arguments:
- queries: bfloat16 [32768, 2560], P(('leaf', 'blk', 'kv')), parts along dimension 0, may hold values from -8 to 8
- keys: bfloat16 [131072, 512], P(('leaf', 'blk', 'kv')), parts along dimension 0, may hold values from -8 to 8
- values: bfloat16 [131072, 512], P(('leaf', 'blk', 'kv')), parts along dimension 0, may hold values from -6 to 6
- ancestry: int32 [256, 64], P('leaf'), parts along dimension 0, may hold values from 0 to 1, as said below
- leaf_tiles: int32 [256], P('leaf'), parts along dimension 0, may hold values from 1 to 63, as said below
Outputs:
- attended: bfloat16 [32768, 2560], P(('leaf', 'blk', 'kv')), parts along dimension 0
The draws below stay inside these ranges and needn't reach their ends.
There are 16 independent parts, one for each index of `leaf`. The reference program is written for one: setup_inputs(seed, part) draws one part's arguments, and reference() takes and returns one part's arrays. A program takes and returns all parts, laid end to end along the dimension named above; each array names one. Nothing has to cross between parts.
Inputs may be any that keep to these rules, and one draw needn't show every extreme that they name: ancestry[a, t] is 1 exactly when key tile t is a strict ancestor of tile leaf_tiles[a] in the tree whose nodes are the key tiles; tile 0 is the root of the tree. `leaf_tiles`: strictly rising; the last entry is 63.
All inputs are finite; a program needn't handle non-finite values.
Results may differ from the reference program's by a relative error of at most 0.018.
Values may be sent and summed in bfloat16 or wider, within the bound.
No kernel may reach another device: no remote copies, remote signals or barrier semaphores. Data moves between devices by JAX's collectives and lax.ppermute only.
A program may use at most 256 MiB of HBM per device.

```python
import jax
import jax.numpy as jnp
from jax import lax

TILE = 128
KV_HEADS = 4
GROUP = 5
DH = 128
QUERIES = 2048
KEYS = 8192
Q_TILES = 16
K_TILES = 64


def tree_shape(key):
    tile_count = K_TILES
    leaf_count = Q_TILES
    window = max(1, K_TILES // 4)
    parent_key = jax.random.fold_in(key, 11)
    leaf_key = jax.random.fold_in(key, 12)
    tile_ids = jnp.arange(tile_count, dtype=jnp.int32)
    lowest = jnp.maximum(tile_ids - window, 0)
    spread = jax.random.randint(parent_key, (tile_count,), 0, 1 << 20, dtype=jnp.int32)
    parent = jnp.where(tile_ids > 0, lowest + spread % jnp.maximum(tile_ids - lowest, 1), 0).astype(jnp.int32)
    shuffled = jax.random.permutation(leaf_key, tile_count - 2).astype(jnp.int32) + 1
    chosen = jnp.sort(shuffled[:leaf_count - 1])
    leaves = jnp.concatenate([chosen, jnp.full((1,), tile_count - 1, jnp.int32)]).astype(jnp.int32)

    def climb_up(index_, carried):
        ancestors, current = carried
        current = parent[current]
        ancestors = jnp.maximum(ancestors, (tile_ids[None, :] == current[:, None]).astype(jnp.int32))
        return (ancestors, current)
    ancestors, _ = lax.fori_loop(0, tile_count, climb_up, (jnp.zeros((leaf_count, tile_count), jnp.int32), leaves))
    return (ancestors, leaves)


def draw_ancestry(key, part):
    ancestors, leaves = tree_shape(key)
    return ancestors


def draw_leaf_tiles(key, part):
    ancestors, leaves = tree_shape(key)
    return leaves


def draw_queries(key, part):
    key = jax.random.fold_in(key, 3)
    shape_all = (QUERIES, KV_HEADS * GROUP * DH)
    result = jax.random.truncated_normal(key, -6.0, 6.0, shape_all, jnp.float32)
    return result.astype(jnp.bfloat16)


def draw_keys(key, part):
    key = jax.random.fold_in(key, 4)
    shape_all = (KEYS, KV_HEADS * DH)
    result = jax.random.truncated_normal(key, -6.0, 6.0, shape_all, jnp.float32)
    return result.astype(jnp.bfloat16)


def level_of(key, shape, pieces, low, high):
    def one(dim, shards_of):
        draws = jax.random.uniform(jax.random.fold_in(jax.random.fold_in(key, 6), dim), (shards_of,), jnp.float32, low / len(pieces), high / len(pieces))
        return jnp.repeat(jnp.exp(draws), shape[dim] // shards_of).reshape((-1,) + (1,) * (len(shape) - dim - 1))

    factor_of = one(*pieces[0])
    for cut in pieces[1:]:
        factor_of = factor_of * one(*cut)
    return factor_of


def normal_values(rng, extent, deviation, reach, pieces=(), kind=jnp.bfloat16):
    loudness = level_of(rng, extent, pieces, -0.22, 0.18) if pieces else 1.0
    drawn = jax.random.normal(rng, extent, jnp.float32) * deviation * loudness
    return jnp.minimum(jnp.maximum(drawn, -reach), reach).astype(kind)


def setup_inputs(seed: int = 0, part: int = 0) -> dict:
    key_list = jax.random.split(jax.random.key(seed), 6)
    part_splits = jax.random.split(jax.random.fold_in(key_list[5], part), 6)
    return {
        "queries": draw_queries(jax.random.fold_in(jax.random.fold_in(key_list[5], part), 71), part),
        "keys": draw_keys(jax.random.fold_in(jax.random.fold_in(key_list[5], part), 71), part),
        "values": normal_values(part_splits[2], (KEYS, KV_HEADS * DH), 1.0, 6.0, ((0, 16),)),
        "ancestry": draw_ancestry(jax.random.fold_in(jax.random.fold_in(key_list[5], part), 71), part),
        "leaf_tiles": draw_leaf_tiles(jax.random.fold_in(jax.random.fold_in(key_list[5], part), 71), part),
    }


def reference(queries, keys, values, ancestry, leaf_tiles):
    query_ids = jnp.arange(QUERIES, dtype=jnp.int32)
    key_ids = jnp.arange(KEYS, dtype=jnp.int32)
    query_tiles = query_ids // TILE
    key_tiles = key_ids // TILE
    own_tile = leaf_tiles[query_tiles]
    linked = ancestry[query_tiles][:, key_tiles] == 1
    causal = (key_ids % TILE)[None, :] <= (query_ids % TILE)[:, None]
    allowed = jnp.where(key_tiles[None, :] == own_tile[:, None], causal, linked)
    query_heads = queries.reshape(QUERIES, KV_HEADS, GROUP, DH)
    key_heads = keys.reshape(KEYS, KV_HEADS, DH)
    value_heads = values.reshape(KEYS, KV_HEADS, DH)
    scaling = 1.0 / jnp.sqrt(jnp.float32(DH))

    def one_head(head_id):
        query_part = query_heads[:, head_id].astype(jnp.float32)
        key_part = key_heads[:, head_id].astype(jnp.float32)
        value_part = value_heads[:, head_id].astype(jnp.float32)
        scores = jnp.einsum('qgd,sd->gqs', query_part, key_part) * scaling
        scores = jnp.where(allowed[None], scores, -1e+30)
        row_peak = lax.optimization_barrier(jnp.max(scores, axis=-1))
        weights = jnp.where(allowed[None], jnp.exp(scores - row_peak[..., None]), 0.0)
        row_total = lax.optimization_barrier(jnp.sum(weights, axis=-1))
        rounded = lax.optimization_barrier(weights.astype(jnp.bfloat16)).astype(jnp.float32)
        summed = jnp.einsum('gqs,sd->qgd', rounded, value_part)
        return summed / jnp.transpose(row_total, (1, 0))[..., None]
    result = lax.map(one_head, jnp.arange(KV_HEADS, dtype=jnp.int32))
    result = jnp.transpose(result, (1, 0, 2, 3)).reshape(QUERIES, KV_HEADS * GROUP * DH)
    return result.astype(jnp.bfloat16)
```

```python
import functools
import math

import jax
import jax.numpy as jnp
from jax import lax
from jax.experimental import pallas as pl
from jax.experimental.pallas import tpu as pltpu
from jax.sharding import PartitionSpec as P

TILE = 128
KV_HEADS = 4
GROUP = 5
DH = 128
WIDE = GROUP * DH
RING = 4
BLKS = 4
LOW = -1e30
SCALE = math.log2(math.e) / math.sqrt(DH)


def pack_kernel(q_ref, k_ref, v_ref, *refs):
    kv_out, q_out = refs[:RING], refs[RING:]
    me = lax.axis_index("kv")
    for step in range(RING):
        head = lax.rem(me + step, RING)
        narrow = pl.ds(pl.multiple_of(head * DH, DH), DH)
        wide = pl.ds(pl.multiple_of(head * WIDE, DH), WIDE)
        kv_out[step][0] = k_ref[:, narrow]
        kv_out[step][1] = v_ref[:, narrow]
        q_out[step][...] = q_ref[:, wide]


def pack(queries, keys, values):
    rows = keys.shape[0]
    vmem = pl.BlockSpec(memory_space=pltpu.VMEM)
    return pl.pallas_call(
        pack_kernel,
        out_shape=[jax.ShapeDtypeStruct((2, rows, DH), jnp.bfloat16)] * RING
        + [jax.ShapeDtypeStruct((TILE, WIDE), jnp.bfloat16)] * RING,
        in_specs=[vmem] * 3,
        out_specs=[vmem] * (2 * RING),
        name="pack",
    )(queries, keys, values)


def unpack_kernel(*refs):
    parts, out_ref = refs[:RING], refs[RING]
    me = lax.axis_index("kv")
    for step in range(RING):
        head = lax.rem(me + step, RING)
        wide = pl.ds(pl.multiple_of(head * WIDE, DH), WIDE)
        out_ref[:, wide] = parts[step][...]


def unpack(parts):
    vmem = pl.BlockSpec(memory_space=pltpu.VMEM)
    return pl.pallas_call(
        unpack_kernel,
        out_shape=jax.ShapeDtypeStruct((TILE, KV_HEADS * WIDE), jnp.bfloat16),
        in_specs=[vmem] * RING,
        out_specs=vmem,
        name="unpack",
    )(*parts)


def attend_kernel(slots_ref, counts_ref, *refs):
    q_refs, kv_refs = refs[:RING], refs[RING : RING + RING * BLKS]
    o_refs = refs[RING + RING * BLKS : 2 * RING + RING * BLKS]
    held, scores, sems = refs[2 * RING + RING * BLKS :]
    copies = [
        pltpu.make_async_copy(kv_refs[i], held.at[i], sems.at[i]) for i in range(RING * BLKS)
    ]
    for copy in copies:
        copy.start()
    for copy in copies:
        copy.wait()
    tiles_each = held.shape[2] // TILE
    ahead = lax.broadcasted_iota(jnp.int32, (TILE, TILE), 1) - lax.broadcasted_iota(
        jnp.int32, (TILE, TILE), 0
    )

    def tile_of(which, slot):
        block = slot // tiles_each
        row = pl.multiple_of((slot % tiles_each) * TILE, TILE)
        return held[block, which, pl.ds(row, TILE), :]

    def pair_of(which, step, pair):
        return jnp.concatenate(
            [tile_of(which, slots_ref[step, 2 * pair]), tile_of(which, slots_ref[step, 2 * pair + 1])], axis=0
        )

    for step in range(RING):
        count = counts_ref[step]
        pairs = (count + 1) // 2
        queries = jnp.concatenate(
            [q_refs[step][:, g * DH : (g + 1) * DH] for g in range(GROUP)], axis=0
        )

        def reach(tile):
            return jnp.where(tile < count - 1, TILE, jnp.where(tile == count - 1, 0, -TILE))

        def first(pair, peak):
            keys = pair_of(0, step, pair)
            raw = lax.dot_general(
                queries, keys, (((1,), (1,)), ((), ())), preferred_element_type=jnp.float32
            )
            for half in range(2):
                allowed = ahead <= reach(2 * pair + half)
                part = raw[:, half * TILE : (half + 1) * TILE].reshape(GROUP, TILE, TILE)
                part = jnp.where(allowed[None], part, LOW).reshape(GROUP * TILE, TILE)
                scores[pair, :, half * TILE : (half + 1) * TILE] = part
                peak = jnp.maximum(peak, part)
            return peak

        peak = lax.fori_loop(0, pairs, first, jnp.full((GROUP * TILE, TILE), LOW, jnp.float32))
        peak = jnp.max(peak, axis=1, keepdims=True) * SCALE

        def second(pair, carried):
            total, summed = carried
            weights = jnp.exp2(scores[pair] * SCALE - peak)
            total = total + weights[:, :TILE] + weights[:, TILE:]
            summed = summed + jnp.dot(
                weights.astype(jnp.bfloat16), pair_of(1, step, pair), preferred_element_type=jnp.float32
            )
            return (total, summed)

        zero = jnp.zeros((GROUP * TILE, TILE), jnp.float32)
        total, summed = lax.fori_loop(0, pairs, second, (zero, zero))
        result = (summed / jnp.sum(total, axis=1, keepdims=True)).astype(jnp.bfloat16)
        for g in range(GROUP):
            o_refs[step][:, g * DH : (g + 1) * DH] = result[g * TILE : (g + 1) * TILE]


def attend(slots, counts, query_parts, kv_parts, key_tiles):
    rows = kv_parts[0].shape[1]
    vmem = pl.BlockSpec(memory_space=pltpu.VMEM)
    smem = pl.BlockSpec(memory_space=pltpu.SMEM)
    return pl.pallas_call(
        attend_kernel,
        out_shape=[jax.ShapeDtypeStruct((TILE, WIDE), jnp.bfloat16)] * RING,
        in_specs=[smem, smem] + [vmem] * RING + [pl.BlockSpec(memory_space=pl.ANY)] * (RING * BLKS),
        out_specs=[vmem] * RING,
        scratch_shapes=[
            pltpu.VMEM((RING * BLKS, 2, rows, DH), jnp.bfloat16),
            pltpu.VMEM(((key_tiles + 1) // 2, GROUP * TILE, 2 * TILE), jnp.float32),
            pltpu.SemaphoreType.DMA((RING * BLKS,)),
        ],
        compiler_params=pltpu.CompilerParams(vmem_limit_bytes=44 * 1024 * 1024),
        cost_estimate=pl.CostEstimate(flops=10**9, bytes_accessed=6 * 10**6, transcendentals=10**6),
        name="attend",
    )(slots, counts, *query_parts, *kv_parts)


def chain_lists(ancestry, leaf_tiles, blk, me):
    tiles = ancestry.shape[1]
    each = tiles // (BLKS * RING)
    rows = blk * RING + (me - jnp.arange(RING, dtype=jnp.int32)) % RING
    picker = rows[:, None] == jnp.arange(ancestry.shape[0], dtype=jnp.int32)[None, :]
    linked = jnp.sum(jnp.where(picker[:, :, None], ancestry[None], 0), axis=1)
    home = jnp.sum(jnp.where(picker, leaf_tiles[None], 0), axis=1)
    tile = jnp.arange(tiles, dtype=jnp.int32)
    owner = tile // each
    place = (((owner // RING) ^ blk) * RING + (me - owner) % RING) * each + tile % each
    counts = jnp.sum(linked, axis=1)
    lower = tile[:, None] < tile[None, :]
    rank = jnp.sum(jnp.where(lower[None], linked[:, :, None], 0), axis=1)
    hit = (linked[:, :, None] == 1) & (rank[:, :, None] == tile[None, None, :])
    slots = jnp.sum(jnp.where(hit, place[None, :, None], 0), axis=1)
    own = jnp.sum(jnp.where(home[:, None] == tile[None, :], place[None], 0), axis=1)
    slots = jnp.where(tile[None, :] == counts[:, None], own[:, None], slots)
    return slots.astype(jnp.int32), (counts + 1).astype(jnp.int32)


def turn(array, by):
    return lax.ppermute(array, "kv", [(i, (i + by) % RING) for i in range(RING)])


def across(array, bit):
    return lax.ppermute(array, "blk", [(i, i ^ bit) for i in range(BLKS)])


def on_device(queries, keys, values, ancestry, leaf_tiles):
    me = lax.axis_index("kv")
    blk = lax.axis_index("blk")
    packed = pack(queries, keys, values)
    kv_sent, q_sent = packed[:RING], packed[RING:]
    slots, counts = chain_lists(ancestry, leaf_tiles, blk, me)
    own = [kv_sent[0], None, None, None]
    order = (0, 1, 3, 2)
    for step in order[1:]:
        own[step] = turn(kv_sent[step], step)
    far = [None] * RING
    for step in order:
        far[step] = across(own[step], 2)
    q_parts = [q_sent[0]] + [turn(q_sent[step], step) for step in range(1, RING)]
    near = [across(part, 1) for part in own]
    diagonal = [across(part, 1) for part in far]
    outs = attend(slots, counts, q_parts, own + near + far + diagonal, ancestry.shape[1])
    back = [outs[0]] + [turn(outs[step], -step) for step in range(1, RING)]
    return unpack(back)


def solution(mesh):
    in_specs = (
        P(("leaf", "blk", "kv"), None),
        P(("leaf", "blk", "kv"), None),
        P(("leaf", "blk", "kv"), None),
        P("leaf", None),
        P("leaf"),
    )
    out_specs = P(("leaf", "blk", "kv"), None)
    return jax.shard_map(
        on_device, mesh=mesh, in_specs=in_specs, out_specs=out_specs, check_vma=False
    )
```

```python
import functools
import math

import jax
import jax.numpy as jnp
from jax import lax
from jax.experimental import pallas as pl
from jax.experimental.pallas import tpu as pltpu
from jax.sharding import PartitionSpec as P

TILE = 128
KV_HEADS = 4
GROUP = 5
DH = 128
WIDE = GROUP * DH
RING = 4
BLKS = 4
LOW = -1e30
SCALE = math.log2(math.e) / math.sqrt(DH)


def in_hbm(array):
    return pltpu.with_memory_space_constraint(array, pltpu.HBM)


def in_vmem(array):
    return pltpu.with_memory_space_constraint(array, pltpu.VMEM)


def pack_kernel(queries_ref, keys_ref, values_ref, here_ref, first_ref, last_ref, third_ref, q1_ref, q3_ref, sems):
    me = lax.axis_index("kv")
    rows = keys_ref.shape[0]
    copies = []

    def move(source, target):
        copies.append(pltpu.make_async_copy(source, target, sems.at[len(copies)]))
        copies[-1].start()

    for step, target in ((1, first_ref), (3, third_ref), (0, here_ref), (2, last_ref)):
        head = lax.rem(me + step, RING)
        narrow = pl.ds(pl.multiple_of(head * DH, DH), DH)
        move(keys_ref.at[:, narrow], target.at[pl.ds(0, rows)])
        move(values_ref.at[:, narrow], target.at[pl.ds(rows, rows)])
    for step, target, start in ((2, last_ref, 2 * rows), (1, q1_ref, 0), (3, q3_ref, 0)):
        head = lax.rem(me + step, RING)
        for g in range(GROUP):
            narrow = pl.ds(pl.multiple_of((head * GROUP + g) * DH, DH), DH)
            move(queries_ref.at[:, narrow], target.at[pl.ds(start + g * TILE, TILE)])
    for copy in copies:
        copy.wait()


def pack(queries, keys, values):
    rows = 2 * keys.shape[0]
    hbm = pl.BlockSpec(memory_space=pltpu.HBM)
    vmem = pl.BlockSpec(memory_space=pltpu.VMEM)
    lengths = (rows, rows, rows + WIDE, rows, WIDE, WIDE)
    return pl.pallas_call(
        pack_kernel,
        out_shape=[pltpu.VMEM((length, DH), jnp.bfloat16) for length in lengths],
        in_specs=[hbm] * 3,
        out_specs=[vmem] * len(lengths),
        scratch_shapes=[pltpu.SemaphoreType.DMA((2 * RING + 3 * GROUP,))],
        compiler_params=pltpu.CompilerParams(vmem_limit_bytes=4 * 1024 * 1024),
        name="pack",
    )(in_hbm(queries), in_hbm(keys), in_hbm(values))


def unpack_kernel(*refs):
    parts, out_ref, sems = refs[1:RING], refs[RING], refs[RING + 1]
    me = lax.axis_index("kv")
    copies = []
    for i in range(RING - 1):
        wide = pl.ds(pl.multiple_of(lax.rem(me + i + 1, RING) * WIDE, DH), WIDE)
        copies.append(pltpu.make_async_copy(parts[i], out_ref.at[:, wide], sems.at[i]))
    for copy in copies:
        copy.start()
    for copy in copies:
        copy.wait()


def unpack(whole, parts):
    hbm = pl.BlockSpec(memory_space=pltpu.HBM)
    vmem = pl.BlockSpec(memory_space=pltpu.VMEM)
    return pl.pallas_call(
        unpack_kernel,
        out_shape=pltpu.HBM((TILE, KV_HEADS * WIDE), jnp.bfloat16),
        in_specs=[hbm] + [vmem] * (RING - 1),
        out_specs=hbm,
        input_output_aliases={0: 0},
        scratch_shapes=[pltpu.SemaphoreType.DMA((RING - 1,))],
        compiler_params=pltpu.CompilerParams(vmem_limit_bytes=4 * 1024 * 1024),
        name="unpack",
    )(in_hbm(whole), *[in_vmem(part) for part in parts])


def attend_kernel(last, parts, table_ref, queries_ref, *refs):
    q_refs, kv_refs, refs = refs[: RING - 1], refs[RING - 1 : RING - 1 + parts], refs[RING - 1 + parts :]
    peak_ref, total_ref, summed_ref = refs[:3]
    o_refs, (held, own_queries, own_held, sems) = refs[3:-4], refs[-4:]
    me = lax.axis_index("kv")
    fetches = []
    for g in range(GROUP):
        narrow = pl.ds(pl.multiple_of((me * GROUP + g) * DH, DH), DH)
        fetches.append(
            pltpu.make_async_copy(queries_ref.at[:, narrow], own_queries.at[pl.ds(g * TILE, TILE)], sems.at[g])
        )
        fetches[-1].start()
    place, rows = 0, held.shape[1]
    for kv_ref in kv_refs:
        for i in range(kv_ref.shape[0] // rows):
            held[place] = kv_ref[i * rows : (i + 1) * rows]
            place += 1
    rows = rows // 2
    tiles_each = rows // TILE
    behind = lax.broadcasted_iota(jnp.int32, (TILE, TILE), 0) - lax.broadcasted_iota(
        jnp.int32, (TILE, TILE), 1
    )

    def tile_of(which, slot):
        block = slot // tiles_each
        row = pl.multiple_of((slot % tiles_each) * TILE, TILE)
        return held[block, pl.ds(row + which * rows, TILE), :]

    for step in (1, 3, 2, 0):
        row = step + RING if last else step
        full, home = table_ref[row, 0], table_ref[row, 1]
        if step == 0:
            for fetch in fetches:
                fetch.wait()
        q_ref = q_refs[step - 1] if step else own_queries
        queries = q_ref[q_ref.shape[0] - WIDE :]

        def visit(masked, pair, carried):
            peak, total, summed = carried
            slots = [table_ref[row, 2 + 2 * pair + half] for half in range(2)]
            keys = jnp.concatenate([tile_of(0, slot) for slot in slots], axis=0)
            raw = lax.dot_general(
                keys, queries, (((1,), (1,)), ((), ())), preferred_element_type=jnp.float32
            )
            if masked:
                halves = []
                for half in range(2):
                    tile = 2 * pair + half
                    reach = jnp.where(tile < full, TILE, jnp.where(tile < full + home, 0, -TILE))
                    allowed = jnp.concatenate([behind <= reach] * GROUP, axis=1)
                    halves.append(jnp.where(allowed, raw[half * TILE : (half + 1) * TILE], LOW))
                raw = jnp.concatenate(halves, axis=0)
            higher = jnp.maximum(peak, jnp.max(raw, axis=0, keepdims=True))
            kept = jnp.exp2((peak - higher) * SCALE)
            weights = jnp.exp2(raw * SCALE - higher * SCALE)
            total = total * kept + jnp.sum(weights, axis=0, keepdims=True)
            value_tiles = jnp.concatenate([tile_of(1, slot) for slot in slots], axis=0)
            update = lax.dot_general(
                value_tiles,
                weights.astype(jnp.bfloat16),
                (((0,), (0,)), ((), ())),
                preferred_element_type=jnp.float32,
            )
            return (higher, total, summed * kept + update)

        if last:
            carried = (peak_ref[step], total_ref[step], summed_ref[step])
        else:
            carried = (
                jnp.full((1, WIDE), LOW, jnp.float32),
                jnp.zeros((1, WIDE), jnp.float32),
                jnp.zeros((DH, WIDE), jnp.float32),
            )
        whole = full // 2
        carried = lax.fori_loop(0, whole, functools.partial(visit, False), carried)
        carried = lax.fori_loop(whole, (full + home + 1) // 2, functools.partial(visit, True), carried)
        peak, total, summed = carried
        if last:
            result = summed / total
            o_ref = o_refs[step] if step else own_held
            for g in range(GROUP):
                o_ref[:, g * DH : (g + 1) * DH] = (
                    result[:, g * TILE : (g + 1) * TILE].T.astype(jnp.bfloat16)
                )
        else:
            peak_ref[step] = peak
            total_ref[step] = total
            summed_ref[step] = summed
    if last:
        wide = pl.ds(pl.multiple_of(me * WIDE, DH), WIDE)
        place_own = pltpu.make_async_copy(own_held, o_refs[0].at[:, wide], sems.at[GROUP])
        place_own.start()
        place_own.wait()


def attend(table, queries, query_parts, kv_parts, state, cost):
    last = state is not None
    rows = kv_parts[0].shape[0]
    vmem = pl.BlockSpec(memory_space=pltpu.VMEM)
    smem = pl.BlockSpec(memory_space=pltpu.SMEM)
    hbm = pl.BlockSpec(memory_space=pltpu.HBM)
    operands = [table, in_hbm(queries), *query_parts, *kv_parts] + (list(state) if last else [])
    in_specs = [smem, hbm] + [vmem] * (len(query_parts) + len(kv_parts))
    state_specs = [vmem] * 3
    if last:
        outs = [pltpu.HBM((TILE, KV_HEADS * WIDE), jnp.bfloat16)]
        outs += [pltpu.VMEM((TILE, WIDE), jnp.bfloat16)] * (RING - 1)
        in_specs += state_specs
        out_specs = [hbm] + [vmem] * (RING - 1)
    else:
        outs = [pltpu.VMEM((RING, rows, WIDE), jnp.float32) for rows in (1, 1, DH)]
        out_specs = state_specs
    return pl.pallas_call(
        functools.partial(attend_kernel, last, len(kv_parts)),
        out_shape=outs,
        in_specs=in_specs,
        out_specs=out_specs,
        scratch_shapes=[
            pltpu.VMEM((2 * RING, rows, DH), jnp.bfloat16),
            pltpu.VMEM((WIDE, DH), jnp.bfloat16),
            pltpu.VMEM((TILE, WIDE), jnp.bfloat16),
            pltpu.SemaphoreType.DMA((GROUP + 1,)),
        ],
        compiler_params=pltpu.CompilerParams(vmem_limit_bytes=12 * 1024 * 1024),
        cost_estimate=pl.CostEstimate(flops=0, bytes_accessed=cost, transcendentals=0),
        name="attend_last" if last else "attend_first",
    )(*operands)


def tables_kernel(ancestry_ref, leaf_tiles_ref, table_ref):
    me, blk = lax.axis_index("kv"), lax.axis_index("blk")
    tiles = ancestry_ref.shape[1]
    each = tiles // (BLKS * RING)
    query_tiles = [blk * RING + lax.rem(me - step + RING, RING) for step in range(RING)]

    def place_of(tile):
        owner = tile // each
        relative = (owner // RING) ^ blk
        turned = (me - owner) & (RING - 1)
        return relative // 2, ((relative & 1) * RING + (turned ^ (turned // 2))) * each + (tile & (each - 1))

    def visit(tile, counts):
        column, place = place_of(tile)
        later = []
        for step in range(RING):
            linked = ancestry_ref[query_tiles[step], tile]
            near, far = counts[2 * step : 2 * step + 2]
            table_ref[step + column * RING, 2 + jnp.where(column == 0, near, far)] = place
            later += [near + linked * (1 - column), far + linked * column]
        return tuple(later)

    def clear(at, carried):
        for row in range(2 * RING):
            table_ref[row, at] = 0
        return carried

    lax.fori_loop(0, table_ref.shape[1], clear, 0)
    counts = lax.fori_loop(0, tiles, visit, (jnp.int32(0),) * (2 * RING))
    for step in range(RING):
        column, place = place_of(leaf_tiles_ref[query_tiles[step]])
        for side in range(2):
            table_ref[step + side * RING, 0] = counts[2 * step + side]
            table_ref[step + side * RING, 1] = jnp.where(column == side, 1, 0)
        table_ref[step + column * RING, 2 + jnp.where(column == 0, counts[2 * step], counts[2 * step + 1])] = place


def chain_tables(ancestry, leaf_tiles):
    smem = pl.BlockSpec(memory_space=pltpu.SMEM)
    return pl.pallas_call(
        tables_kernel,
        out_shape=jax.ShapeDtypeStruct((2 * RING, ancestry.shape[1] // 2 + 8), jnp.int32),
        in_specs=[smem, smem],
        out_specs=smem,
        compiler_params=pltpu.CompilerParams(vmem_limit_bytes=1024 * 1024),
        cost_estimate=pl.CostEstimate(flops=0, bytes_accessed=10**8, transcendentals=0),
        name="tables",
    )(ancestry, leaf_tiles)


def turn(array, by):
    return lax.ppermute(array, "kv", [(i, (i + by) % RING) for i in range(RING)])


def across(array, bit):
    return lax.ppermute(array, "blk", [(i, i ^ bit) for i in range(BLKS)])


def on_device(queries, keys, values, ancestry, leaf_tiles):
    table = chain_tables(ancestry, leaf_tiles)
    own_here, sent_first, sent_last, sent_third, q_first, q_third = pack(queries, keys, values)

    first, third, far_here = turn(sent_first, 1), turn(sent_third, 3), across(own_here, 2)
    own_sides = jnp.concatenate([first, third], axis=0)
    own_sides, far_here, sent_last, q_first, q_third, table = lax.optimization_barrier(
        (own_sides, far_here, sent_last, q_first, q_third, table)
    )

    far_sides, own_last = across(own_sides, 2), turn(sent_last, 2)
    q_first, q_third = turn(q_first, 1), turn(q_third, 3)
    own_here, own_sides, own_last, far_here, far_sides, q_first, q_third = lax.optimization_barrier(
        (own_here, own_sides, own_last, far_here, far_sides, q_first, q_third)
    )

    far_last = across(own_last[: own_here.shape[0]], 2)
    near_here, near_sides, near_last = across(own_here, 1), across(own_sides, 1), across(own_last, 1)
    diagonal_here, diagonal_sides = across(far_here, 1), across(far_sides, 1)
    q_parts = [q_first, own_last, q_third]
    near_parts = [own_here, own_sides, own_last, near_here, near_sides, near_last]
    state = attend(table, queries, q_parts, near_parts, None, 10**8)
    far_last, *state = lax.optimization_barrier((far_last, *state))

    diagonal_last = across(far_last, 1)
    far_parts = [far_here, far_sides, far_last, diagonal_here, diagonal_sides, diagonal_last]
    whole, *outs = attend(table, queries, q_parts, far_parts, state, 10**7)
    return unpack(whole, [turn(outs[i], -1 - i) for i in range(RING - 1)])


def solution(mesh):
    in_specs = (
        P(("leaf", "blk", "kv"), None),
        P(("leaf", "blk", "kv"), None),
        P(("leaf", "blk", "kv"), None),
        P("leaf", None),
        P("leaf"),
    )
    out_specs = P(("leaf", "blk", "kv"), None)
    return jax.shard_map(
        on_device, mesh=mesh, in_specs=in_specs, out_specs=out_specs, check_vma=False
    )
```

```python
import functools
import math

import jax
import jax.numpy as jnp
from jax import lax
from jax.experimental import pallas as pl
from jax.experimental.pallas import tpu as pltpu
from jax.sharding import PartitionSpec as P

TILE = 128
KV_HEADS = 4
GROUP = 5
DH = 128
WIDE = GROUP * DH
RING = 4
BLKS = 4
LOW = -1e30
SCALE = math.log2(math.e) / math.sqrt(DH)


def in_hbm(array):
    return pltpu.with_memory_space_constraint(array, pltpu.HBM)


def in_vmem(array):
    return pltpu.with_memory_space_constraint(array, pltpu.VMEM)


def pack_kernel(queries_ref, keys_ref, values_ref, across_ref, first_ref, third_ref, q_ref, sems):
    me = lax.axis_index("kv")
    rows = keys_ref.shape[0]
    copies = []

    def move(source, target):
        copies.append(pltpu.make_async_copy(source, target, sems.at[len(copies)]))
        copies[-1].start()

    for step, target, start in ((0, across_ref, 0), (2, across_ref, 2 * rows), (1, first_ref, 0), (3, third_ref, 0)):
        head = lax.rem(me + step, RING)
        narrow = pl.ds(pl.multiple_of(head * DH, DH), DH)
        move(keys_ref.at[:, narrow], target.at[pl.ds(start, rows)])
        move(values_ref.at[:, narrow], target.at[pl.ds(start + rows, rows)])
    for step, target, start in ((1, first_ref, 2 * rows), (3, third_ref, 2 * rows), (2, q_ref, 0)):
        head = lax.rem(me + step, RING)
        for g in range(GROUP):
            narrow = pl.ds(pl.multiple_of((head * GROUP + g) * DH, DH), DH)
            move(queries_ref.at[:, narrow], target.at[pl.ds(start + g * TILE, TILE)])
    for copy in copies:
        copy.wait()


def pack(queries, keys, values):
    rows = 2 * keys.shape[0]
    hbm = pl.BlockSpec(memory_space=pltpu.HBM)
    vmem = pl.BlockSpec(memory_space=pltpu.VMEM)
    lengths = (2 * rows, rows + WIDE, rows + WIDE, WIDE)
    return pl.pallas_call(
        pack_kernel,
        out_shape=[pltpu.VMEM((length, DH), jnp.bfloat16) for length in lengths],
        in_specs=[hbm] * 3,
        out_specs=[vmem] * len(lengths),
        scratch_shapes=[pltpu.SemaphoreType.DMA((2 * RING + 3 * GROUP,))],
        compiler_params=pltpu.CompilerParams(vmem_limit_bytes=4 * 1024 * 1024),
        name="pack",
    )(in_hbm(queries), in_hbm(keys), in_hbm(values))


def unpack_kernel(*refs):
    parts, out_ref, sems = refs[1:RING], refs[RING], refs[RING + 1]
    me = lax.axis_index("kv")
    copies = []
    for i in range(RING - 1):
        wide = pl.ds(pl.multiple_of(lax.rem(me + i + 1, RING) * WIDE, DH), WIDE)
        copies.append(pltpu.make_async_copy(parts[i], out_ref.at[:, wide], sems.at[i]))
    for copy in copies:
        copy.start()
    for copy in copies:
        copy.wait()


def unpack(whole, parts):
    hbm = pl.BlockSpec(memory_space=pltpu.HBM)
    vmem = pl.BlockSpec(memory_space=pltpu.VMEM)
    return pl.pallas_call(
        unpack_kernel,
        out_shape=pltpu.HBM((TILE, KV_HEADS * WIDE), jnp.bfloat16),
        in_specs=[hbm] + [vmem] * (RING - 1),
        out_specs=hbm,
        input_output_aliases={0: 0},
        scratch_shapes=[pltpu.SemaphoreType.DMA((RING - 1,))],
        compiler_params=pltpu.CompilerParams(vmem_limit_bytes=4 * 1024 * 1024),
        name="unpack",
    )(in_hbm(whole), *[in_vmem(part) for part in parts])


def attend_kernel(steps, last, parts, table_ref, queries_ref, *refs):
    passed = [step for step in steps if step]
    q_refs = dict(zip(passed, refs))
    refs = refs[len(passed) :]
    kv_refs, refs = refs[:parts], refs[parts:]
    if last:
        before, o_refs, refs = refs[:3], refs[3 : 3 + len(steps)], refs[3 + len(steps) :]
        held, own_queries, own_held, peaks, totals, sums, sems = refs
    else:
        peaks, totals, sums, held, own_queries, own_held, sems = refs
    me = lax.axis_index("kv")
    fetches = []
    if 0 in steps:
        q_refs[0] = own_queries
        for g in range(GROUP):
            narrow = pl.ds(pl.multiple_of((me * GROUP + g) * DH, DH), DH)
            fetches.append(
                pltpu.make_async_copy(queries_ref.at[:, narrow], own_queries.at[pl.ds(g * TILE, TILE)], sems.at[g])
            )
            fetches[-1].start()
    place, rows = 0, held.shape[1]
    for kv_ref in kv_refs:
        for i in range(kv_ref.shape[0] // rows):
            held[place] = kv_ref[i * rows : (i + 1) * rows]
            place += 1
    rows = rows // 2
    tiles_each = rows // TILE
    ahead = lax.broadcasted_iota(jnp.int32, (TILE, TILE), 0) > lax.broadcasted_iota(jnp.int32, (TILE, TILE), 1)
    ahead = jnp.concatenate([ahead] * GROUP, axis=1)
    for fetch in fetches:
        fetch.wait()

    def tiles_of(which, slots):
        found = []
        for slot in slots:
            row = pl.multiple_of((slot % tiles_each) * TILE, TILE)
            found.append(held[slot // tiles_each, pl.ds(row + which * rows, TILE), :])
        return jnp.concatenate(found, axis=0)

    def visit(step, slots, shown, own, carried):
        peak, total, summed = carried
        q_ref = q_refs[step]
        raw = lax.dot_general(
            tiles_of(0, slots),
            q_ref[q_ref.shape[0] - WIDE :],
            (((1,), (1,)), ((), ())),
            preferred_element_type=jnp.float32,
        )
        if own:
            raw = jnp.where(ahead, LOW, raw)
        raw = [raw[i * TILE : (i + 1) * TILE] for i in range(len(slots))]
        higher = peak
        for part, show in zip(raw, shown):
            higher = jnp.maximum(higher, jnp.where(show, jnp.max(part, axis=0, keepdims=True), LOW))
        shift = higher * SCALE
        kept = jnp.exp2(peak * SCALE - shift)
        weights = [jnp.exp2(part * SCALE - jnp.where(show, shift, -LOW)) for part, show in zip(raw, shown)]
        total = total * kept
        for part in weights:
            total = total + jnp.sum(part, axis=0, keepdims=True)
        update = lax.dot_general(
            tiles_of(1, slots),
            jnp.concatenate(weights, axis=0).astype(jnp.bfloat16),
            (((0,), (0,)), ((), ())),
            preferred_element_type=jnp.float32,
        )
        return (higher, total, summed * kept + update)

    for i, step in enumerate(steps):
        row = step + RING if last else step
        if last:
            carried = tuple(ref[step] for ref in before)
        else:
            carried = (
                jnp.full((1, WIDE), LOW, jnp.float32),
                jnp.zeros((1, WIDE), jnp.float32),
                jnp.zeros((DH, WIDE), jnp.float32),
            )
        carried = visit(step, [table_ref[row, 2]], [table_ref[row, 1] == 1], True, carried)
        for ref, value in zip((peaks, totals, sums), carried):
            ref[i] = value

    fulls = [table_ref[step + RING if last else step, 0] for step in steps]
    most = functools.reduce(jnp.maximum, fulls)

    def round_of(start, width, at, carry):
        for i, (step, full) in enumerate(zip(steps, fulls)):
            row = step + RING if last else step
            tiles = [start + width * at + place for place in range(width)]
            slots = [table_ref[row, 3 + tile] for tile in tiles]
            shown = [tile < full for tile in tiles]
            carried = visit(step, slots, shown, False, (peaks[i], totals[i], sums[i]))
            for ref, value in zip((peaks, totals, sums), carried):
                ref[i] = value
        return carry

    fours = (most + 1) // 4
    lax.fori_loop(0, fours, functools.partial(round_of, 0, 4), 0)
    lax.fori_loop(0, (most - 4 * fours + 1) // 2, functools.partial(round_of, 4 * fours, 2), 0)

    if last:
        for i, (step, o_ref) in enumerate(zip(steps, o_refs)):
            result = sums[i] / totals[i]
            target = o_ref if step else own_held
            for g in range(GROUP):
                target[:, g * DH : (g + 1) * DH] = result[:, g * TILE : (g + 1) * TILE].T.astype(jnp.bfloat16)
            if step == 0:
                wide = pl.ds(pl.multiple_of(me * WIDE, DH), WIDE)
                place_own = pltpu.make_async_copy(own_held, o_ref.at[:, wide], sems.at[GROUP])
                place_own.start()
                place_own.wait()


def attend(steps, table, queries, query_parts, kv_parts, state, cost):
    last = state is not None
    rows = 2 * TILE * 4
    blocks = sum(part.shape[0] // rows for part in kv_parts)
    vmem = pl.BlockSpec(memory_space=pltpu.VMEM)
    smem = pl.BlockSpec(memory_space=pltpu.SMEM)
    hbm = pl.BlockSpec(memory_space=pltpu.HBM)
    operands = [table, in_hbm(queries), *[query_parts[step] for step in steps if step], *kv_parts]
    operands += list(state) if last else []
    in_specs = [smem, hbm] + [vmem] * (len(operands) - 2)
    state_shapes = [pltpu.VMEM((len(steps), length, WIDE), jnp.float32) for length in (1, 1, DH)]
    if last:
        outs = [
            pltpu.VMEM((TILE, WIDE), jnp.bfloat16)
            if step
            else pltpu.HBM((TILE, KV_HEADS * WIDE), jnp.bfloat16)
            for step in steps
        ]
        out_specs = [vmem if step else hbm for step in steps]
    else:
        outs, out_specs = state_shapes, [vmem] * 3
    return pl.pallas_call(
        functools.partial(attend_kernel, steps, last, len(kv_parts)),
        out_shape=outs,
        in_specs=in_specs,
        out_specs=out_specs,
        scratch_shapes=[
            pltpu.VMEM((blocks, rows, DH), jnp.bfloat16),
            pltpu.VMEM((WIDE, DH), jnp.bfloat16),
            pltpu.VMEM((TILE, WIDE), jnp.bfloat16),
            *(state_shapes if last else []),
            pltpu.SemaphoreType.DMA((GROUP + 1,)),
        ],
        compiler_params=pltpu.CompilerParams(vmem_limit_bytes=12 * 1024 * 1024),
        cost_estimate=pl.CostEstimate(flops=0, bytes_accessed=cost, transcendentals=0),
        name="attend_last" if last else "attend_first",
    )(*operands)


def tables_kernel(ancestry_ref, leaf_tiles_ref, table_ref):
    me, blk = lax.axis_index("kv"), lax.axis_index("blk")
    tiles = ancestry_ref.shape[1]
    each = tiles // (BLKS * RING)
    query_tiles = [blk * RING + lax.rem(me - step + RING, RING) for step in range(RING)]

    def place_of(tile):
        owner = tile // each
        relative = (owner // RING) ^ blk
        turned = (me - owner) & (RING - 1)
        low, high = relative & 1, relative // 2
        late = jnp.where((turned == 2) | ((turned != 0) & (high == 1)), 1, 0)
        early_block = low * RING + jnp.where(turned == 0, high, 2 + turned // 2)
        late_block = low * 2 + jnp.where(turned == 2, RING + high, turned // 2)
        block = jnp.where(late == 1, late_block, early_block)
        return late, block * each + (tile & (each - 1))

    def visit(tile, counts):
        late, place = place_of(tile)
        later = []
        for step in range(RING):
            linked = ancestry_ref[query_tiles[step], tile]
            early_count, late_count = counts[2 * step : 2 * step + 2]
            table_ref[step + late * RING, 3 + jnp.where(late == 1, late_count, early_count)] = place
            later += [early_count + linked * (1 - late), late_count + linked * late]
        return tuple(later)

    def clear(at, carried):
        for row in range(2 * RING):
            table_ref[row, at] = 0
        return carried

    lax.fori_loop(0, table_ref.shape[1], clear, 0)
    counts = lax.fori_loop(0, tiles, visit, (jnp.int32(0),) * (2 * RING))
    for step in range(RING):
        late, place = place_of(leaf_tiles_ref[query_tiles[step]])
        for side in range(2):
            table_ref[step + side * RING, 0] = counts[2 * step + side]
            table_ref[step + side * RING, 1] = jnp.where(late == side, 1, 0)
            table_ref[step + side * RING, 2] = jnp.where(late == side, place, 0)


def chain_tables(ancestry, leaf_tiles):
    smem = pl.BlockSpec(memory_space=pltpu.SMEM)
    return pl.pallas_call(
        tables_kernel,
        out_shape=jax.ShapeDtypeStruct((2 * RING, ancestry.shape[1] + 8), jnp.int32),
        in_specs=[smem, smem],
        out_specs=smem,
        compiler_params=pltpu.CompilerParams(vmem_limit_bytes=1024 * 1024),
        cost_estimate=pl.CostEstimate(flops=0, bytes_accessed=10**8, transcendentals=0),
        name="tables",
    )(ancestry, leaf_tiles)


def turn(array, by):
    return lax.ppermute(array, "kv", [(i, (i + by) % RING) for i in range(RING)])


def across(array, bit):
    return lax.ppermute(array, "blk", [(i, i ^ bit) for i in range(BLKS)])


def on_device(queries, keys, values, ancestry, leaf_tiles):
    table = chain_tables(ancestry, leaf_tiles)
    sent_across, sent_first, sent_third, sent_queries = pack(queries, keys, values)
    block = 2 * keys.shape[0]

    got_across = across(sent_across, 2)
    got_first, got_third = turn(sent_first, 1), turn(sent_third, 3)
    got_queries = turn(sent_queries, 2)
    sent_across, got_across, got_first, got_third, got_queries, table = lax.optimization_barrier(
        (sent_across, got_across, got_first, got_third, got_queries, table)
    )
    query_parts = {1: got_first, 2: got_queries, 3: got_third}

    own_sides = jnp.concatenate([got_first[:block], got_third[:block]], axis=0)
    far_sides = across(own_sides, 2)
    got_last = turn(jnp.concatenate([sent_across[block:], got_across[block:]], axis=0), 2)
    here = jnp.concatenate([sent_across[:block], got_across[:block]], axis=0)
    swapped_here, near_sides = across(here, 1), across(own_sides, 1)
    parts = [here, own_sides, swapped_here, near_sides]
    state = attend((0, 1, 2, 3), table, queries, query_parts, parts, None, 10**8)
    far_sides, got_last, *state = lax.optimization_barrier((far_sides, got_last, *state))

    diagonal_sides, swapped_last = across(far_sides, 1), across(got_last, 1)
    parts = [far_sides, diagonal_sides, got_last, swapped_last]
    out_first, out_third = attend((1, 3), table, queries, query_parts, parts, state, 10**8)
    back_first, back_third = turn(out_first, -1), turn(out_third, -3)
    table, *state = lax.optimization_barrier((out_first, table, *state))[1:]
    out_second, whole = attend((2, 0), table, queries, query_parts, parts, state, 10**8)
    out_second, back_first, back_third = lax.optimization_barrier((out_second, back_first, back_third))
    return unpack(whole, [back_first, turn(out_second, -2), back_third])


def solution(mesh):
    in_specs = (
        P(("leaf", "blk", "kv"), None),
        P(("leaf", "blk", "kv"), None),
        P(("leaf", "blk", "kv"), None),
        P("leaf", None),
        P("leaf"),
    )
    out_specs = P(("leaf", "blk", "kv"), None)
    return jax.shard_map(
        on_device, mesh=mesh, in_specs=in_specs, out_specs=out_specs, check_vma=False
    )
```

```python
import functools
import math

import jax
import jax.numpy as jnp
from jax import lax
from jax.experimental import pallas as pl
from jax.experimental.pallas import tpu as pltpu
from jax.sharding import PartitionSpec as P

TILE = 128
KV_HEADS = 4
GROUP = 5
DH = 128
WIDE = GROUP * DH
RING = 4
BLKS = 4
GROUPS = 3
LOW = -1e30
SCALE = math.log2(math.e) / math.sqrt(DH)


def in_hbm(array):
    return pltpu.with_memory_space_constraint(array, pltpu.HBM)


def in_vmem(array):
    return pltpu.with_memory_space_constraint(array, pltpu.VMEM)


def pack_kernel(queries_ref, keys_ref, values_ref, across_ref, first_ref, third_ref, q_ref, sems):
    me = lax.axis_index("kv")
    rows = keys_ref.shape[0]
    copies = []

    def move(source, target):
        copies.append(pltpu.make_async_copy(source, target, sems.at[len(copies)]))
        copies[-1].start()

    for step, target, start in ((0, across_ref, 0), (2, across_ref, 2 * rows), (1, first_ref, 0), (3, third_ref, 0)):
        head = lax.rem(me + step, RING)
        narrow = pl.ds(pl.multiple_of(head * DH, DH), DH)
        move(keys_ref.at[:, narrow], target.at[pl.ds(start, rows)])
        move(values_ref.at[:, narrow], target.at[pl.ds(start + rows, rows)])
    for step, target, start in ((1, first_ref, 2 * rows), (3, third_ref, 2 * rows), (2, q_ref, 0)):
        head = lax.rem(me + step, RING)
        for g in range(GROUP):
            narrow = pl.ds(pl.multiple_of((head * GROUP + g) * DH, DH), DH)
            move(queries_ref.at[:, narrow], target.at[pl.ds(start + g * TILE, TILE)])
    for copy in copies:
        copy.wait()


def pack(queries, keys, values):
    rows = 2 * keys.shape[0]
    hbm = pl.BlockSpec(memory_space=pltpu.HBM)
    vmem = pl.BlockSpec(memory_space=pltpu.VMEM)
    lengths = (2 * rows, rows + WIDE, rows + WIDE, WIDE)
    return pl.pallas_call(
        pack_kernel,
        out_shape=[pltpu.VMEM((length, DH), jnp.bfloat16) for length in lengths],
        in_specs=[hbm] * 3,
        out_specs=[vmem] * len(lengths),
        scratch_shapes=[pltpu.SemaphoreType.DMA((2 * RING + 3 * GROUP,))],
        compiler_params=pltpu.CompilerParams(vmem_limit_bytes=4 * 1024 * 1024),
        name="pack",
    )(in_hbm(queries), in_hbm(keys), in_hbm(values))


def unpack_kernel(*refs):
    parts, out_ref, sems = refs[:RING], refs[RING], refs[RING + 1]
    me = lax.axis_index("kv")
    copies = []
    for step in range(RING):
        wide = pl.ds(pl.multiple_of(lax.rem(me + step, RING) * WIDE, DH), WIDE)
        copies.append(pltpu.make_async_copy(parts[step], out_ref.at[:, wide], sems.at[step]))
    for copy in copies:
        copy.start()
    for copy in copies:
        copy.wait()


def unpack(parts):
    return pl.pallas_call(
        unpack_kernel,
        out_shape=pltpu.HBM((TILE, KV_HEADS * WIDE), jnp.bfloat16),
        in_specs=[pl.BlockSpec(memory_space=pltpu.VMEM)] * RING,
        out_specs=pl.BlockSpec(memory_space=pltpu.HBM),
        scratch_shapes=[pltpu.SemaphoreType.DMA((RING,))],
        compiler_params=pltpu.CompilerParams(vmem_limit_bytes=4 * 1024 * 1024),
        name="unpack",
    )(*[in_vmem(part) for part in parts])


def attend_kernel(group, parts, table_ref, *refs):
    q_refs, refs = list(refs[:RING]), refs[RING:]
    kv_refs, refs = refs[:parts], refs[parts:]
    fetches = []
    if group == 0:
        peaks, totals, sums, own_queries, held, sems = refs
        me = lax.axis_index("kv")
        for g in range(GROUP):
            narrow = pl.ds(pl.multiple_of((me * GROUP + g) * DH, DH), DH)
            fetches.append(
                pltpu.make_async_copy(q_refs[0].at[:, narrow], own_queries.at[pl.ds(g * TILE, TILE)], sems.at[g])
            )
            fetches[-1].start()
        q_refs[0] = own_queries
    else:
        (peaks, totals, sums), o_refs, held = refs[3:6], refs[6:-1], refs[-1]
    place, rows = 0, held.shape[1]
    for kv_ref in kv_refs:
        for i in range(kv_ref.shape[0] // rows):
            held[place] = kv_ref[i * rows : (i + 1) * rows]
            place += 1
    rows = rows // 2
    tiles_each = rows // TILE
    ahead = lax.broadcasted_iota(jnp.int32, (TILE, TILE), 0) > lax.broadcasted_iota(jnp.int32, (TILE, TILE), 1)
    ahead = jnp.concatenate([ahead] * GROUP, axis=1)
    for fetch in fetches:
        fetch.wait()

    def tiles_of(which, slots):
        found = []
        for slot in slots:
            row = pl.multiple_of((slot % tiles_each) * TILE, TILE)
            found.append(held[slot // tiles_each, pl.ds(row + which * rows, TILE), :])
        return jnp.concatenate(found, axis=0)

    def visit(step, slots, shown, own, carried):
        peak, total, summed = carried
        q_ref = q_refs[step]
        raw = lax.dot_general(
            tiles_of(0, slots),
            q_ref[q_ref.shape[0] - WIDE :],
            (((1,), (1,)), ((), ())),
            preferred_element_type=jnp.float32,
        )
        if own:
            raw = jnp.where(ahead, LOW, raw)
        raw = [raw[i * TILE : (i + 1) * TILE] for i in range(len(slots))]
        higher = peak
        for part, show in zip(raw, shown):
            higher = jnp.maximum(higher, jnp.where(show, jnp.max(part, axis=0, keepdims=True), LOW))
        shift = higher * SCALE
        kept = jnp.exp2(peak * SCALE - shift)
        weights = [jnp.exp2(part * SCALE - jnp.where(show, shift, -LOW)) for part, show in zip(raw, shown)]
        total = total * kept
        for part in weights:
            total = total + jnp.sum(part, axis=0, keepdims=True)
        update = lax.dot_general(
            tiles_of(1, slots),
            jnp.concatenate(weights, axis=0).astype(jnp.bfloat16),
            (((0,), (0,)), ((), ())),
            preferred_element_type=jnp.float32,
        )
        return (higher, total, summed * kept + update)

    def add(step, slots, shown, own):
        carried = visit(step, slots, shown, own, (peaks[step], totals[step], sums[step]))
        for ref, value in zip((peaks, totals, sums), carried):
            ref[step] = value

    if group == 0:
        peaks[...] = jnp.full(peaks.shape, LOW, jnp.float32)
        totals[...] = jnp.zeros(totals.shape, jnp.float32)
        sums[...] = jnp.zeros(sums.shape, jnp.float32)
    for step in range(RING):
        row = step + RING * group
        if group == 0:
            add(step, [table_ref[row, 2]], [table_ref[row, 1] == 1], True)
        else:
            pl.when(table_ref[row, 1] == 1)(functools.partial(add, step, [table_ref[row, 2]], [True], True))

    fulls = [table_ref[step + RING * group, 0] for step in range(RING)]
    most = functools.reduce(jnp.maximum, fulls)

    def round_of(start, width, at, carry):
        for step in range(RING):
            tiles = [start + width * at + place for place in range(width)]
            slots = [table_ref[step + RING * group, 3 + tile] for tile in tiles]
            add(step, slots, [tile < fulls[step] for tile in tiles], False)
        return carry

    fours = (most + 1) // 4
    lax.fori_loop(0, fours, functools.partial(round_of, 0, 4), 0)
    lax.fori_loop(0, (most - 4 * fours + 1) // 2, functools.partial(round_of, 4 * fours, 2), 0)

    if group == GROUPS - 1:
        for step in range(RING):
            result = sums[step] / totals[step]
            for g in range(GROUP):
                o_refs[step][:, g * DH : (g + 1) * DH] = (
                    result[:, g * TILE : (g + 1) * TILE].T.astype(jnp.bfloat16)
                )


def attend(group, table, query_parts, kv_parts, state, cost):
    rows = 2 * TILE * 4
    blocks = sum(part.shape[0] // rows for part in kv_parts)
    vmem = pl.BlockSpec(memory_space=pltpu.VMEM)
    smem = pl.BlockSpec(memory_space=pltpu.SMEM)
    hbm = pl.BlockSpec(memory_space=pltpu.HBM)
    operands = [table, *query_parts, *kv_parts, *state]
    in_specs = [smem] + [vmem] * (len(operands) - 1)
    outs = [pltpu.VMEM((RING, length, WIDE), jnp.float32) for length in (1, 1, DH)]
    scratch = [pltpu.VMEM((blocks, rows, DH), jnp.bfloat16)]
    aliases = {}
    if group == 0:
        operands[1], in_specs[1] = in_hbm(query_parts[0]), hbm
        outs.append(pltpu.VMEM((WIDE, DH), jnp.bfloat16))
        scratch.append(pltpu.SemaphoreType.DMA((GROUP,)))
    else:
        aliases = {len(operands) - 3 + i: i for i in range(3)}
    if group == GROUPS - 1:
        outs += [pltpu.VMEM((TILE, WIDE), jnp.bfloat16)] * RING
    return pl.pallas_call(
        functools.partial(attend_kernel, group, len(kv_parts)),
        out_shape=outs,
        in_specs=in_specs,
        out_specs=[vmem] * len(outs),
        input_output_aliases=aliases,
        scratch_shapes=scratch,
        compiler_params=pltpu.CompilerParams(vmem_limit_bytes=12 * 1024 * 1024),
        cost_estimate=pl.CostEstimate(flops=0, bytes_accessed=cost, transcendentals=0),
        name="attend",
    )(*operands)


def tables_kernel(ancestry_ref, leaf_tiles_ref, table_ref):
    me, blk = lax.axis_index("kv"), lax.axis_index("blk")
    tiles = ancestry_ref.shape[1]
    each = tiles // (BLKS * RING)
    query_tiles = [blk * RING + lax.rem(me - step + RING, RING) for step in range(RING)]

    def place_of(tile):
        owner = tile // each
        relative = (owner // RING) ^ blk
        turned = (me - owner) & (RING - 1)
        low, high = relative & 1, relative // 2
        early = (turned == 0) | ((high == 0) & (turned != 2))
        middle = (low == 0) & (turned != 2)
        group = jnp.where(early, 0, jnp.where(middle, 1, 2))
        early_block = low * RING + jnp.where(turned == 0, high, 2 + turned // 2)
        late_block = jnp.where(turned == 2, 2 + low * 2 + high, turned // 2)
        block = jnp.where(early, early_block, late_block)
        return group * RING, block * each + (tile & (each - 1))

    def visit(tile, carried):
        row, place = place_of(tile)
        for step in range(RING):
            count = table_ref[row + step, 0]
            table_ref[row + step, 3 + count] = place
            table_ref[row + step, 0] = count + ancestry_ref[query_tiles[step], tile]
        return carried

    def clear(at, carried):
        for row in range(GROUPS * RING):
            table_ref[row, at] = 0
        return carried

    lax.fori_loop(0, table_ref.shape[1], clear, 0)
    lax.fori_loop(0, tiles, visit, 0)
    for step in range(RING):
        row, place = place_of(leaf_tiles_ref[query_tiles[step]])
        table_ref[row + step, 1] = 1
        table_ref[row + step, 2] = place


def chain_tables(ancestry, leaf_tiles):
    smem = pl.BlockSpec(memory_space=pltpu.SMEM)
    return pl.pallas_call(
        tables_kernel,
        out_shape=jax.ShapeDtypeStruct((GROUPS * RING, ancestry.shape[1] // 2 + 8), jnp.int32),
        in_specs=[smem, smem],
        out_specs=smem,
        compiler_params=pltpu.CompilerParams(vmem_limit_bytes=1024 * 1024),
        cost_estimate=pl.CostEstimate(flops=0, bytes_accessed=10**8, transcendentals=0),
        name="tables",
    )(ancestry, leaf_tiles)


def turn(array, by):
    return lax.ppermute(array, "kv", [(i, (i + by) % RING) for i in range(RING)])


def across(array, bit):
    return lax.ppermute(array, "blk", [(i, i ^ bit) for i in range(BLKS)])


def on_device(queries, keys, values, ancestry, leaf_tiles):
    table = chain_tables(ancestry, leaf_tiles)
    sent_across, sent_first, sent_third, sent_queries = pack(queries, keys, values)
    block = 2 * keys.shape[0]

    got_first, got_third = turn(sent_first, 1), turn(sent_third, 3)
    got_across = across(sent_across, 2)
    got_queries = turn(sent_queries, 2)
    sent_across, got_across, got_first, got_third, got_queries, table = lax.optimization_barrier(
        (sent_across, got_across, got_first, got_third, got_queries, table)
    )
    query_parts = [queries, got_first, got_queries, got_third]

    got_last = turn(jnp.concatenate([sent_across[block:], got_across[block:]], axis=0), 2)
    own_sides = jnp.concatenate([got_first[:block], got_third[:block]], axis=0)
    far_sides = across(own_sides, 2)
    here = jnp.concatenate([sent_across[:block], got_across[:block]], axis=0)
    swapped_here, near_sides = across(here, 1), across(own_sides, 1)
    parts = [here, own_sides, swapped_here, near_sides]
    *state, query_parts[0] = attend(0, table, query_parts, parts, [], 10**8)

    far_sides, *state = lax.optimization_barrier((far_sides, *state))
    diagonal_sides = across(far_sides, 1)
    state = attend(1, table, query_parts, [far_sides], state, 10)
    got_last, *state = lax.optimization_barrier((got_last, *state))
    outs = attend(2, table, query_parts, [diagonal_sides, got_last, across(got_last, 1)], state, 10)[3:]
    return unpack([outs[0]] + [turn(outs[step], -step) for step in range(1, RING)])


def solution(mesh):
    in_specs = (
        P(("leaf", "blk", "kv"), None),
        P(("leaf", "blk", "kv"), None),
        P(("leaf", "blk", "kv"), None),
        P("leaf", None),
        P("leaf"),
    )
    out_specs = P(("leaf", "blk", "kv"), None)
    return jax.shard_map(
        on_device, mesh=mesh, in_specs=in_specs, out_specs=out_specs, check_vma=False
    )
```

```python
import functools
import math

import jax
import jax.numpy as jnp
from jax import lax
from jax.experimental import pallas as pl
from jax.experimental.pallas import tpu as pltpu
from jax.sharding import PartitionSpec as P

TILE = 128
KV_HEADS = 4
GROUP = 5
DH = 128
WIDE = GROUP * DH
RING = 4
BLKS = 4
GROUPS = 3
LOW = -1e30
SCALE = math.log2(math.e) / math.sqrt(DH)


def in_hbm(array):
    return pltpu.with_memory_space_constraint(array, pltpu.HBM)


def in_vmem(array):
    return pltpu.with_memory_space_constraint(array, pltpu.VMEM)


def pack_kernel(queries_ref, keys_ref, values_ref, here_ref, opposite_ref, first_ref, third_ref, q_ref, sems):
    me = lax.axis_index("kv")
    rows = keys_ref.shape[0]
    copies = []

    def move(source, target):
        copies.append(pltpu.make_async_copy(source, target, sems.at[len(copies)]))
        copies[-1].start()

    for step, target in ((1, first_ref), (3, third_ref), (0, here_ref), (2, opposite_ref)):
        head = lax.rem(me + step, RING)
        narrow = pl.ds(pl.multiple_of(head * DH, DH), DH)
        move(keys_ref.at[:, narrow], target.at[pl.ds(0, rows)])
        move(values_ref.at[:, narrow], target.at[pl.ds(rows, rows)])
    for step, target, start in ((1, first_ref, 2 * rows), (3, third_ref, 2 * rows), (2, q_ref, 0)):
        head = lax.rem(me + step, RING)
        for g in range(GROUP):
            narrow = pl.ds(pl.multiple_of((head * GROUP + g) * DH, DH), DH)
            move(queries_ref.at[:, narrow], target.at[pl.ds(start + g * TILE, TILE)])
    for copy in copies:
        copy.wait()


def pack(queries, keys, values):
    rows = 2 * keys.shape[0]
    hbm = pl.BlockSpec(memory_space=pltpu.HBM)
    vmem = pl.BlockSpec(memory_space=pltpu.VMEM)
    lengths = (rows, rows, rows + WIDE, rows + WIDE, WIDE)
    return pl.pallas_call(
        pack_kernel,
        out_shape=[pltpu.VMEM((length, DH), jnp.bfloat16) for length in lengths],
        in_specs=[hbm] * 3,
        out_specs=[vmem] * len(lengths),
        scratch_shapes=[pltpu.SemaphoreType.DMA((2 * RING + 3 * GROUP,))],
        compiler_params=pltpu.CompilerParams(vmem_limit_bytes=4 * 1024 * 1024),
        name="pack",
    )(in_hbm(queries), in_hbm(keys), in_hbm(values))


def unpack_kernel(*refs):
    parts, out_ref, sems = refs[:RING], refs[RING], refs[RING + 1]
    me = lax.axis_index("kv")
    copies = []
    for step in range(RING):
        wide = pl.ds(pl.multiple_of(lax.rem(me + step, RING) * WIDE, DH), WIDE)
        copies.append(pltpu.make_async_copy(parts[step], out_ref.at[:, wide], sems.at[step]))
    for copy in copies:
        copy.start()
    for copy in copies:
        copy.wait()


def unpack(parts):
    return pl.pallas_call(
        unpack_kernel,
        out_shape=pltpu.HBM((TILE, KV_HEADS * WIDE), jnp.bfloat16),
        in_specs=[pl.BlockSpec(memory_space=pltpu.VMEM)] * RING,
        out_specs=pl.BlockSpec(memory_space=pltpu.HBM),
        scratch_shapes=[pltpu.SemaphoreType.DMA((RING,))],
        compiler_params=pltpu.CompilerParams(vmem_limit_bytes=4 * 1024 * 1024),
        name="unpack",
    )(*[in_vmem(part) for part in parts])


def attend_kernel(group, parts, table_ref, *refs):
    q_refs, refs = list(refs[:RING]), refs[RING:]
    kv_refs, refs = refs[:parts], refs[parts:]
    fetches = []
    if group == 0:
        peaks, totals, sums, own_queries, held, sems = refs
        me = lax.axis_index("kv")
        for g in range(GROUP):
            narrow = pl.ds(pl.multiple_of((me * GROUP + g) * DH, DH), DH)
            fetches.append(
                pltpu.make_async_copy(q_refs[0].at[:, narrow], own_queries.at[pl.ds(g * TILE, TILE)], sems.at[g])
            )
            fetches[-1].start()
        q_refs[0] = own_queries
    else:
        (peaks, totals, sums), o_refs, held = refs[3:6], refs[6:-1], refs[-1]
    place, rows = 0, held.shape[1]
    for kv_ref in kv_refs:
        for i in range(kv_ref.shape[0] // rows):
            held[place] = kv_ref[i * rows : (i + 1) * rows]
            place += 1
    rows = rows // 2
    tiles_each = rows // TILE
    ahead = lax.broadcasted_iota(jnp.int32, (TILE, TILE), 0) > lax.broadcasted_iota(jnp.int32, (TILE, TILE), 1)
    ahead = jnp.concatenate([ahead] * GROUP, axis=1)
    for fetch in fetches:
        fetch.wait()

    def tiles_of(which, slots):
        found = []
        for slot in slots:
            row = pl.multiple_of((slot % tiles_each) * TILE, TILE)
            found.append(held[slot // tiles_each, pl.ds(row + which * rows, TILE), :])
        return jnp.concatenate(found, axis=0)

    def visit(step, slots, shown, own, carried):
        peak, total, summed = carried
        q_ref = q_refs[step]
        raw = lax.dot_general(
            tiles_of(0, slots),
            q_ref[q_ref.shape[0] - WIDE :],
            (((1,), (1,)), ((), ())),
            preferred_element_type=jnp.float32,
        )
        if own:
            raw = jnp.where(ahead, LOW, raw)
        raw = [raw[i * TILE : (i + 1) * TILE] for i in range(len(slots))]
        higher = peak
        for part, show in zip(raw, shown):
            higher = jnp.maximum(higher, jnp.where(show, jnp.max(part, axis=0, keepdims=True), LOW))
        shift = higher * SCALE
        kept = jnp.exp2(peak * SCALE - shift)
        weights = [jnp.exp2(part * SCALE - jnp.where(show, shift, -LOW)) for part, show in zip(raw, shown)]
        total = total * kept
        for part in weights:
            total = total + jnp.sum(part, axis=0, keepdims=True)
        update = lax.dot_general(
            tiles_of(1, slots),
            jnp.concatenate(weights, axis=0).astype(jnp.bfloat16),
            (((0,), (0,)), ((), ())),
            preferred_element_type=jnp.float32,
        )
        return (higher, total, summed * kept + update)

    def add(step, slots, shown, own):
        carried = visit(step, slots, shown, own, (peaks[step], totals[step], sums[step]))
        for ref, value in zip((peaks, totals, sums), carried):
            ref[step] = value

    if group == 0:
        peaks[...] = jnp.full(peaks.shape, LOW, jnp.float32)
        totals[...] = jnp.zeros(totals.shape, jnp.float32)
        sums[...] = jnp.zeros(sums.shape, jnp.float32)
    for step in range(RING):
        row = step + RING * group
        if group == 0:
            add(step, [table_ref[row, 2]], [table_ref[row, 1] == 1], True)
        else:
            pl.when(table_ref[row, 1] == 1)(functools.partial(add, step, [table_ref[row, 2]], [True], True))

    def round_of(steps, start, width, at, carry):
        for step in steps:
            tiles = [start + width * at + place for place in range(width)]
            slots = [table_ref[step + RING * group, 3 + tile] for tile in tiles]
            add(step, slots, [tile < table_ref[step + RING * group, 0] for tile in tiles], False)
        return carry

    for steps in ((0, 1), (2, 3)):
        most = functools.reduce(jnp.maximum, [table_ref[step + RING * group, 0] for step in steps])
        fours = (most + 1) // 4
        lax.fori_loop(0, fours, functools.partial(round_of, steps, 0, 4), 0)
        lax.fori_loop(0, (most - 4 * fours + 1) // 2, functools.partial(round_of, steps, 4 * fours, 2), 0)

    if group == GROUPS - 1:
        for step in range(RING):
            result = sums[step] * (1.0 / totals[step])
            for g in range(GROUP):
                o_refs[step][:, g * DH : (g + 1) * DH] = (
                    result[:, g * TILE : (g + 1) * TILE].T.astype(jnp.bfloat16)
                )


def attend(group, table, query_parts, kv_parts, state, cost):
    rows = 2 * TILE * 4
    blocks = sum(part.shape[0] // rows for part in kv_parts)
    vmem = pl.BlockSpec(memory_space=pltpu.VMEM)
    smem = pl.BlockSpec(memory_space=pltpu.SMEM)
    hbm = pl.BlockSpec(memory_space=pltpu.HBM)
    operands = [table, *query_parts, *kv_parts, *state]
    in_specs = [smem] + [vmem] * (len(operands) - 1)
    outs = [pltpu.VMEM((RING, length, WIDE), jnp.float32) for length in (1, 1, DH)]
    scratch = [pltpu.VMEM((blocks, rows, DH), jnp.bfloat16)]
    aliases = {}
    if group == 0:
        operands[1], in_specs[1] = in_hbm(query_parts[0]), hbm
        outs.append(pltpu.VMEM((WIDE, DH), jnp.bfloat16))
        scratch.append(pltpu.SemaphoreType.DMA((GROUP,)))
    else:
        aliases = {len(operands) - 3 + i: i for i in range(3)}
    if group == GROUPS - 1:
        outs += [pltpu.VMEM((TILE, WIDE), jnp.bfloat16)] * RING
    return pl.pallas_call(
        functools.partial(attend_kernel, group, len(kv_parts)),
        out_shape=outs,
        in_specs=in_specs,
        out_specs=[vmem] * len(outs),
        input_output_aliases=aliases,
        scratch_shapes=scratch,
        compiler_params=pltpu.CompilerParams(vmem_limit_bytes=12 * 1024 * 1024),
        cost_estimate=pl.CostEstimate(flops=0, bytes_accessed=cost, transcendentals=0),
        name="attend",
    )(*operands)


def tables_kernel(ancestry_ref, leaf_tiles_ref, table_ref):
    me, blk = lax.axis_index("kv"), lax.axis_index("blk")
    tiles = ancestry_ref.shape[1]
    each = tiles // (BLKS * RING)
    query_tiles = [blk * RING + lax.rem(me - step + RING, RING) for step in range(RING)]

    def place_of(tile):
        owner = tile // each
        relative = (owner // RING) ^ blk
        turned = (me - owner) & (RING - 1)
        low, high = relative & 1, relative // 2
        early = (turned == 0) | ((high == 0) & (turned != 2))
        middle = (low == 0) & (turned != 2)
        group = jnp.where(early, 0, jnp.where(middle, 1, 2))
        early_block = low * RING + jnp.where(turned == 0, high, 2 + turned // 2)
        late_block = jnp.where(turned == 2, 2 + low * 2 + high, turned // 2)
        block = jnp.where(early, early_block, late_block)
        return group * RING, block * each + (tile & (each - 1))

    def visit(tile, carried):
        row, place = place_of(tile)
        for step in range(RING):
            count = table_ref[row + step, 0]
            table_ref[row + step, 3 + count] = place
            table_ref[row + step, 0] = count + ancestry_ref[query_tiles[step], tile]
        return carried

    def clear(at, carried):
        for row in range(GROUPS * RING):
            table_ref[row, at] = 0
        return carried

    lax.fori_loop(0, table_ref.shape[1], clear, 0)
    lax.fori_loop(0, tiles, visit, 0)
    for step in range(RING):
        row, place = place_of(leaf_tiles_ref[query_tiles[step]])
        table_ref[row + step, 1] = 1
        table_ref[row + step, 2] = place


def chain_tables(ancestry, leaf_tiles):
    smem = pl.BlockSpec(memory_space=pltpu.SMEM)
    return pl.pallas_call(
        tables_kernel,
        out_shape=jax.ShapeDtypeStruct((GROUPS * RING, ancestry.shape[1] // 2 + 8), jnp.int32),
        in_specs=[smem, smem],
        out_specs=smem,
        compiler_params=pltpu.CompilerParams(vmem_limit_bytes=1024 * 1024),
        cost_estimate=pl.CostEstimate(flops=0, bytes_accessed=10**8, transcendentals=0),
        name="tables",
    )(ancestry, leaf_tiles)


def turn(array, by):
    return lax.ppermute(array, "kv", [(i, (i + by) % RING) for i in range(RING)])


def across(array, bit):
    return lax.ppermute(array, "blk", [(i, i ^ bit) for i in range(BLKS)])


def on_device(queries, keys, values, ancestry, leaf_tiles):
    table = chain_tables(ancestry, leaf_tiles)
    sent_here, sent_opposite, sent_first, sent_third, sent_queries = pack(queries, keys, values)
    block = 2 * keys.shape[0]

    got_first, got_third = turn(sent_first, 1), turn(sent_third, 3)
    got_here, got_opposite = across(sent_here, 2), across(sent_opposite, 2)
    got_queries = turn(sent_queries, 2)
    got_first, got_third, got_queries, got_here, got_opposite, sent_here, sent_opposite, table = (
        lax.optimization_barrier(
            (got_first, got_third, got_queries, got_here, got_opposite, sent_here, sent_opposite, table)
        )
    )
    query_parts = [queries, got_first, got_queries, got_third]

    got_last = turn(jnp.concatenate([sent_opposite, got_opposite], axis=0), 2)
    own_sides = jnp.concatenate([got_first[:block], got_third[:block]], axis=0)
    far_sides = across(own_sides, 2)
    here = jnp.concatenate([sent_here, got_here], axis=0)
    swapped_here, near_sides = across(here, 1), across(own_sides, 1)
    parts = [here, own_sides, swapped_here, near_sides]
    *state, query_parts[0] = attend(0, table, query_parts, parts, [], 10**8)

    far_sides, *state = lax.optimization_barrier((far_sides, *state))
    diagonal_sides = across(far_sides, 1)
    state = attend(1, table, query_parts, [far_sides], state, 10)
    got_last, *state = lax.optimization_barrier((got_last, *state))
    outs = attend(2, table, query_parts, [diagonal_sides, got_last, across(got_last, 1)], state, 10)[3:]
    return unpack([outs[0]] + [turn(outs[step], -step) for step in range(1, RING)])


def solution(mesh):
    in_specs = (
        P(("leaf", "blk", "kv"), None),
        P(("leaf", "blk", "kv"), None),
        P(("leaf", "blk", "kv"), None),
        P("leaf", None),
        P("leaf"),
    )
    out_specs = P(("leaf", "blk", "kv"), None)
    return jax.shard_map(
        on_device, mesh=mesh, in_specs=in_specs, out_specs=out_specs, check_vma=False
    )
```

```python
import functools
import math

import jax
import jax.numpy as jnp
from jax import lax
from jax.experimental import pallas as pl
from jax.experimental.pallas import tpu as pltpu
from jax.sharding import PartitionSpec as P

TILE = 128
KV_HEADS = 4
GROUP = 5
DH = 128
WIDE = GROUP * DH
RING = 4
BLKS = 4
GROUPS = 3
LOW = -1e30
SCALE = math.log2(math.e) / math.sqrt(DH)


def in_hbm(array):
    return pltpu.with_memory_space_constraint(array, pltpu.HBM)


def in_vmem(array):
    return pltpu.with_memory_space_constraint(array, pltpu.VMEM)


def pack_kernel(queries_ref, keys_ref, values_ref, here_ref, opposite_ref, first_ref, third_ref, q_ref, sems):
    me = lax.axis_index("kv")
    rows = keys_ref.shape[0]
    copies = []

    def move(source, target):
        copies.append(pltpu.make_async_copy(source, target, sems.at[len(copies)]))
        copies[-1].start()

    for step, target in ((1, first_ref), (3, third_ref), (0, here_ref), (2, opposite_ref)):
        head = lax.rem(me + step, RING)
        narrow = pl.ds(pl.multiple_of(head * DH, DH), DH)
        move(keys_ref.at[:, narrow], target.at[pl.ds(0, rows)])
        move(values_ref.at[:, narrow], target.at[pl.ds(rows, rows)])
    for step, target, start in ((1, first_ref, 2 * rows), (3, third_ref, 2 * rows), (2, q_ref, 0)):
        head = lax.rem(me + step, RING)
        for g in range(GROUP):
            narrow = pl.ds(pl.multiple_of((head * GROUP + g) * DH, DH), DH)
            move(queries_ref.at[:, narrow], target.at[pl.ds(start + g * TILE, TILE)])
    for copy in copies:
        copy.wait()


def pack(queries, keys, values):
    rows = 2 * keys.shape[0]
    hbm = pl.BlockSpec(memory_space=pltpu.HBM)
    vmem = pl.BlockSpec(memory_space=pltpu.VMEM)
    lengths = (rows, rows, rows + WIDE, rows + WIDE, WIDE)
    return pl.pallas_call(
        pack_kernel,
        out_shape=[pltpu.VMEM((length, DH), jnp.bfloat16) for length in lengths],
        in_specs=[hbm] * 3,
        out_specs=[vmem] * len(lengths),
        scratch_shapes=[pltpu.SemaphoreType.DMA((2 * RING + 3 * GROUP,))],
        compiler_params=pltpu.CompilerParams(vmem_limit_bytes=4 * 1024 * 1024),
        name="pack",
    )(in_hbm(queries), in_hbm(keys), in_hbm(values))


def unpack_kernel(*refs):
    parts, out_ref, sems = refs[:RING], refs[RING], refs[RING + 1]
    me = lax.axis_index("kv")
    copies = []
    for step in range(RING):
        wide = pl.ds(pl.multiple_of(lax.rem(me + step, RING) * WIDE, DH), WIDE)
        copies.append(pltpu.make_async_copy(parts[step], out_ref.at[:, wide], sems.at[step]))
    for copy in copies:
        copy.start()
    for copy in copies:
        copy.wait()


def unpack(parts):
    return pl.pallas_call(
        unpack_kernel,
        out_shape=pltpu.HBM((TILE, KV_HEADS * WIDE), jnp.bfloat16),
        in_specs=[pl.BlockSpec(memory_space=pltpu.VMEM)] * RING,
        out_specs=pl.BlockSpec(memory_space=pltpu.HBM),
        scratch_shapes=[pltpu.SemaphoreType.DMA((RING,))],
        compiler_params=pltpu.CompilerParams(vmem_limit_bytes=4 * 1024 * 1024),
        name="unpack",
    )(*[in_vmem(part) for part in parts])


def attend_kernel(group, parts, table_ref, *refs):
    q_refs, refs = list(refs[:RING]), refs[RING:]
    kv_refs, refs = refs[:parts], refs[parts:]
    fetches = []
    if group == 0:
        peaks, totals, sums, own_queries, held, sems = refs
        me = lax.axis_index("kv")
        for g in range(GROUP):
            narrow = pl.ds(pl.multiple_of((me * GROUP + g) * DH, DH), DH)
            fetches.append(
                pltpu.make_async_copy(q_refs[0].at[:, narrow], own_queries.at[pl.ds(g * TILE, TILE)], sems.at[g])
            )
            fetches[-1].start()
        q_refs[0] = own_queries
    else:
        (peaks, totals, sums), o_refs, held = refs[3:6], refs[6:-1], refs[-1]
    place, rows = 0, held.shape[1]
    for kv_ref in kv_refs:
        for i in range(kv_ref.shape[0] // rows):
            held[place] = kv_ref[i * rows : (i + 1) * rows]
            place += 1
    rows = rows // 2
    tiles_each = rows // TILE
    ahead = lax.broadcasted_iota(jnp.int32, (TILE, TILE), 0) > lax.broadcasted_iota(jnp.int32, (TILE, TILE), 1)
    ahead = jnp.concatenate([ahead] * GROUP, axis=1)
    for fetch in fetches:
        fetch.wait()

    def tiles_of(which, slots):
        found = []
        for slot in slots:
            row = pl.multiple_of((slot % tiles_each) * TILE, TILE)
            found.append(held[slot // tiles_each, pl.ds(row + which * rows, TILE), :])
        return jnp.concatenate(found, axis=0)

    def visit(step, slots, shown, own, carried):
        peak, total, summed = carried
        q_ref = q_refs[step]
        raw = lax.dot_general(
            tiles_of(0, slots),
            q_ref[q_ref.shape[0] - WIDE :],
            (((1,), (1,)), ((), ())),
            preferred_element_type=jnp.float32,
        )
        if own:
            raw = jnp.where(ahead, LOW, raw)
        raw = [raw[i * TILE : (i + 1) * TILE] for i in range(len(slots))]
        higher = peak
        for part, show in zip(raw, shown):
            higher = jnp.maximum(higher, jnp.where(show, jnp.max(part, axis=0, keepdims=True), LOW))
        shift = higher * SCALE
        kept = jnp.exp2(peak * SCALE - shift)
        weights = [jnp.exp2(part * SCALE - jnp.where(show, shift, -LOW)) for part, show in zip(raw, shown)]
        total = total * kept
        for part in weights:
            total = total + jnp.sum(part, axis=0, keepdims=True)
        update = lax.dot_general(
            tiles_of(1, slots),
            jnp.concatenate(weights, axis=0).astype(jnp.bfloat16),
            (((0,), (0,)), ((), ())),
            preferred_element_type=jnp.float32,
        )
        return (higher, total, summed * kept + update)

    def add(step, slots, shown, own):
        carried = visit(step, slots, shown, own, (peaks[step], totals[step], sums[step]))
        for ref, value in zip((peaks, totals, sums), carried):
            ref[step] = value

    if group == 0:
        peaks[...] = jnp.full(peaks.shape, LOW, jnp.float32)
        totals[...] = jnp.zeros(totals.shape, jnp.float32)
        sums[...] = jnp.zeros(sums.shape, jnp.float32)
    for step in range(RING):
        row = step + RING * group
        if group == 0:
            add(step, [table_ref[row, 2]], [table_ref[row, 1] == 1], True)
        else:
            pl.when(table_ref[row, 1] == 1)(functools.partial(add, step, [table_ref[row, 2]], [True], True))

    def round_of(steps, start, width, at, carry):
        for step in steps:
            tiles = [start + width * at + place for place in range(width)]
            slots = [table_ref[step + RING * group, 3 + tile] for tile in tiles]
            add(step, slots, [tile < table_ref[step + RING * group, 0] for tile in tiles], False)
        return carry

    for steps in ((0, 1), (2, 3)):
        most = functools.reduce(jnp.maximum, [table_ref[step + RING * group, 0] for step in steps])
        fours = (most + 1) // 4
        lax.fori_loop(0, fours, functools.partial(round_of, steps, 0, 4), 0)
        lax.fori_loop(0, (most - 4 * fours + 1) // 2, functools.partial(round_of, steps, 4 * fours, 2), 0)

    if group == GROUPS - 1:
        for step in range(RING):
            result = (sums[step] * (1.0 / totals[step])).astype(jnp.bfloat16)
            for g in range(GROUP):
                o_refs[step][:, g * DH : (g + 1) * DH] = (
                    result[:, g * TILE : (g + 1) * TILE].T
                )


def attend(group, table, query_parts, kv_parts, state, cost):
    rows = 2 * TILE * 4
    blocks = sum(part.shape[0] // rows for part in kv_parts)
    vmem = pl.BlockSpec(memory_space=pltpu.VMEM)
    smem = pl.BlockSpec(memory_space=pltpu.SMEM)
    hbm = pl.BlockSpec(memory_space=pltpu.HBM)
    operands = [table, *query_parts, *kv_parts, *state]
    in_specs = [smem] + [vmem] * (len(operands) - 1)
    outs = [pltpu.VMEM((RING, length, WIDE), jnp.float32) for length in (1, 1, DH)]
    scratch = [pltpu.VMEM((blocks, rows, DH), jnp.bfloat16)]
    aliases = {}
    if group == 0:
        operands[1], in_specs[1] = in_hbm(query_parts[0]), hbm
        outs.append(pltpu.VMEM((WIDE, DH), jnp.bfloat16))
        scratch.append(pltpu.SemaphoreType.DMA((GROUP,)))
    else:
        aliases = {len(operands) - 3 + i: i for i in range(3)}
    if group == GROUPS - 1:
        outs += [pltpu.VMEM((TILE, WIDE), jnp.bfloat16)] * RING
    return pl.pallas_call(
        functools.partial(attend_kernel, group, len(kv_parts)),
        out_shape=outs,
        in_specs=in_specs,
        out_specs=[vmem] * len(outs),
        input_output_aliases=aliases,
        scratch_shapes=scratch,
        compiler_params=pltpu.CompilerParams(vmem_limit_bytes=12 * 1024 * 1024),
        cost_estimate=pl.CostEstimate(flops=0, bytes_accessed=cost, transcendentals=0),
        name="attend",
    )(*operands)


def tables_kernel(ancestry_ref, leaf_tiles_ref, table_ref):
    me, blk = lax.axis_index("kv"), lax.axis_index("blk")
    tiles = ancestry_ref.shape[1]
    each = tiles // (BLKS * RING)
    query_tiles = [blk * RING + lax.rem(me - step + RING, RING) for step in range(RING)]

    def place_of(tile):
        owner = tile // each
        relative = (owner // RING) ^ blk
        turned = (me - owner) & (RING - 1)
        low, high = relative & 1, relative // 2
        early = (turned == 0) | ((high == 0) & (turned != 2))
        middle = (low == 0) & (turned != 2)
        group = jnp.where(early, 0, jnp.where(middle, 1, 2))
        early_block = low * RING + jnp.where(turned == 0, high, 2 + turned // 2)
        late_block = jnp.where(turned == 2, 2 + low * 2 + high, turned // 2)
        block = jnp.where(early, early_block, late_block)
        return group * RING, block * each + (tile & (each - 1))

    def visit(tile, carried):
        row, place = place_of(tile)
        for step in range(RING):
            count = table_ref[row + step, 0]
            table_ref[row + step, 3 + count] = place
            table_ref[row + step, 0] = count + ancestry_ref[query_tiles[step], tile]
        return carried

    def clear(at, carried):
        for row in range(GROUPS * RING):
            table_ref[row, at] = 0
        return carried

    lax.fori_loop(0, table_ref.shape[1], clear, 0)
    lax.fori_loop(0, tiles, visit, 0)
    for step in range(RING):
        row, place = place_of(leaf_tiles_ref[query_tiles[step]])
        table_ref[row + step, 1] = 1
        table_ref[row + step, 2] = place


def chain_tables(ancestry, leaf_tiles):
    smem = pl.BlockSpec(memory_space=pltpu.SMEM)
    return pl.pallas_call(
        tables_kernel,
        out_shape=jax.ShapeDtypeStruct((GROUPS * RING, ancestry.shape[1] // 2 + 8), jnp.int32),
        in_specs=[smem, smem],
        out_specs=smem,
        compiler_params=pltpu.CompilerParams(vmem_limit_bytes=1024 * 1024),
        cost_estimate=pl.CostEstimate(flops=0, bytes_accessed=10**8, transcendentals=0),
        name="tables",
    )(ancestry, leaf_tiles)


def turn(array, by):
    return lax.ppermute(array, "kv", [(i, (i + by) % RING) for i in range(RING)])


def across(array, bit):
    return lax.ppermute(array, "blk", [(i, i ^ bit) for i in range(BLKS)])


def on_device(queries, keys, values, ancestry, leaf_tiles):
    table = chain_tables(ancestry, leaf_tiles)
    sent_here, sent_opposite, sent_first, sent_third, sent_queries = pack(queries, keys, values)
    block = 2 * keys.shape[0]

    got_first, got_third = turn(sent_first, 1), turn(sent_third, 3)
    got_here, got_opposite = across(sent_here, 2), across(sent_opposite, 2)
    got_queries = turn(sent_queries, 2)
    got_first, got_third, got_queries, got_here, got_opposite, sent_here, sent_opposite, table = (
        lax.optimization_barrier(
            (got_first, got_third, got_queries, got_here, got_opposite, sent_here, sent_opposite, table)
        )
    )
    query_parts = [queries, got_first, got_queries, got_third]

    got_last = turn(jnp.concatenate([sent_opposite, got_opposite], axis=0), 2)
    own_sides = jnp.concatenate([got_first[:block], got_third[:block]], axis=0)
    far_sides = across(own_sides, 2)
    here = jnp.concatenate([sent_here, got_here], axis=0)
    swapped_here, near_sides = across(here, 1), across(own_sides, 1)
    parts = [here, own_sides, swapped_here, near_sides]
    *state, query_parts[0] = attend(0, table, query_parts, parts, [], 10**8)

    far_sides, *state = lax.optimization_barrier((far_sides, *state))
    diagonal_sides = across(far_sides, 1)
    state = attend(1, table, query_parts, [far_sides], state, 10)
    got_last, *state = lax.optimization_barrier((got_last, *state))
    outs = attend(2, table, query_parts, [diagonal_sides, got_last, across(got_last, 1)], state, 10)[3:]
    return unpack([outs[0]] + [turn(outs[step], -step) for step in range(1, RING)])


def solution(mesh):
    in_specs = (
        P(("leaf", "blk", "kv"), None),
        P(("leaf", "blk", "kv"), None),
        P(("leaf", "blk", "kv"), None),
        P("leaf", None),
        P("leaf"),
    )
    out_specs = P(("leaf", "blk", "kv"), None)
    return jax.shard_map(
        on_device, mesh=mesh, in_specs=in_specs, out_specs=out_specs, check_vma=False
    )
```
